128 devices in a mesh: grp: 4 (over z_lo, core), fsdp: 32 (over y, x, z_hi).
Axes of the slice: x: 4, y: 4, z: 4 (z_hi: 2, z_lo: 2; z = z_hi * 2 + z_lo), core: 2. Of those that a mesh axis runs over, the one named last changes fastest.
Arguments:
- activations: bfloat16 [32768, 8192], P(('grp', 'fsdp')), may hold values from -6 to 6
- out_grads: bfloat16 [32768, 14336], P(('grp', 'fsdp')), may hold values from -0.03125 to 0.03125
- basis: bfloat16 [8192, 512], P('fsdp'), may hold values from -0.0625 to 0.0625
- first_moment: float32 [14336, 512], P('fsdp'), may hold values from -6 to 6
- second_moment: float32 [14336, 512], P('fsdp'), may hold values from 0.5 to 2
Outputs:
- update: bfloat16 [8192, 14336], P('fsdp')
- new_first: float32 [14336, 512], P('fsdp')
- new_second: float32 [14336, 512], P('fsdp')
The draws below stay inside these ranges and needn't reach their ends.
All inputs are finite; a program needn't handle non-finite values.
Results may differ from the reference program's by a relative error of at most 0.011.
Values may be sent and summed in bfloat16 or wider, within the bound.
No kernel may reach another device: no remote copies, remote signals or barrier semaphores. Data moves between devices by JAX's collectives and lax.ppermute only.
A program may use at most 128 MiB of HBM per device.

```python
import math
import jax
import jax.numpy as jnp
from jax import lax

D = 8192
FFW = 14336
RANK = 512
STEP = 10
TOK_DEV = 256
TOKENS = 32768
N_GRP = 4
N_FSDP = 32


def levels(rng, dims, cuts, low, high):
    level, own = 1.0, jax.random.fold_in(rng, 6)
    for dim, shards_of in cuts:
        steps = jnp.exp(jax.random.uniform(jax.random.fold_in(own, dim), (shards_of,), jnp.float32, low / len(cuts), high / len(cuts)))
        level = level * jnp.repeat(steps, dims[dim] // shards_of).reshape([-1 if axis == dim else 1 for axis in range(len(dims))])
    return level


def centred(key, shape, spread, limit, split=(), dtype=jnp.bfloat16):
    level = levels(key, shape, split, -0.22, 0.18) if split else 1.0
    array = jax.random.normal(key, shape, jnp.float32) * spread * level
    return jnp.minimum(jnp.maximum(array, -limit), limit).astype(dtype)


def setup_inputs(seed: int = 0) -> dict:
    key_list = jax.random.split(jax.random.key(seed), 6)
    return {
        "activations": centred(key_list[0], (TOKENS, D), 1.0, 6.0, ((0, 128),)),
        "out_grads": centred(key_list[1], (TOKENS, FFW), TOKENS ** -0.5, 0.03125, ((0, 128),)),
        "basis": centred(key_list[2], (D, RANK), D ** -0.5, 0.0625, ((0, 32),)),
        "first_moment": centred(key_list[3], (FFW, RANK), 1.0, 6.0, ((0, 32),), jnp.float32),
        "second_moment": jnp.clip(jnp.exp(math.log(2.0) - 1.3862944 * jax.random.uniform(key_list[4], (FFW, RANK), jnp.float32) ** levels(key_list[4], (FFW, RANK), ((0, 32),), -0.2, 0.2)), 0.5, 2.0),
    }


beta_one = 0.9
beta_two = 0.99
eps = 1e-08
galore_scale = 4.0

def reference(activations, out_grads, basis, first_moment, second_moment):
    projected = jnp.dot(activations, basis, preferred_element_type=jnp.float32).astype(jnp.bfloat16)
    blocks = N_GRP * N_FSDP
    proj_blocks = projected.reshape(blocks, TOK_DEV, RANK)
    grad_blocks = out_grads.reshape(blocks, TOK_DEV, FFW)

    def add_block(running, pair):
        proj_rows, grad_rows = pair
        term_value = lax.dot_general(grad_rows, proj_rows, (((0,), (0,)), ((), ())), preferred_element_type=jnp.float32)
        rounded = lax.optimization_barrier(term_value.astype(jnp.bfloat16))
        return (running + rounded.astype(jnp.float32), None)
    reduced, _ = lax.scan(add_block, jnp.zeros((FFW, RANK), jnp.float32), (proj_blocks, grad_blocks))
    new_first = beta_one * first_moment + (1.0 - beta_one) * reduced
    new_second = beta_two * second_moment + (1.0 - beta_two) * reduced * reduced
    corrected = new_first / (1.0 - beta_one ** STEP)
    normalized = (corrected / (jnp.sqrt(new_second / (1.0 - beta_two ** STEP)) + eps)).astype(jnp.bfloat16)
    expanded = lax.dot_general(basis, normalized, (((1,), (1,)), ((), ())), preferred_element_type=jnp.float32)
    update = (-galore_scale * expanded).astype(jnp.bfloat16)
    return (update, new_first, new_second)
```

```python
import functools

import jax
import jax.numpy as jnp
from jax import lax
from jax.experimental import pallas as pl
from jax.experimental.pallas import tpu as pltpu
from jax.sharding import PartitionSpec as P

STEP = 10


beta_one = 0.9
beta_two = 0.99
eps = 1e-08
galore_scale = 4.0

AXES = ("grp", "fsdp")
BF = jnp.bfloat16
F32 = jnp.float32
ORDERS = (("y", "z", "x"), ("z", "x", "y"), ("x", "y", "z"))


def flat(co):
    z, c = co["z"] % 4, co["c"] % 2
    return ((z % 2) * 2 + c) * 32 + ((co["y"] % 4) * 4 + co["x"] % 4) * 2 + z // 2


def permute(arr, move):
    pairs = []
    for c in range(2):
        for y in range(4):
            for x in range(4):
                for z in range(4):
                    co = {"c": c, "y": y, "x": x, "z": z}
                    pairs.append((flat(co), flat(move(dict(co)))))
    return lax.ppermute(arr, AXES, pairs)


def shift(arr, axis, k):
    def move(co):
        co[axis] += k * (1 - 2 * co["c"])
        return co

    return permute(arr, move)


def swap_core(arr):
    def move(co):
        co["c"] = 1 - co["c"]
        return co

    return permute(arr, move)


def swap_low(arr):
    def move(co):
        co["z"] = co["z"] ^ 1
        return co

    return permute(arr, move)


def place(blocks, where, shape, at):
    n = len(blocks)

    def kernel(where_ref, *refs):
        out, sem = refs[n], refs[n + 1]
        copies = [
            pltpu.make_async_copy(refs[i], out.at[at(i, where_ref)], sem.at[i]) for i in range(n)
        ]
        for copy in copies:
            copy.start()
        for copy in copies:
            copy.wait()

    return pl.pallas_call(
        kernel,
        out_shape=jax.ShapeDtypeStruct(shape, blocks[0].dtype),
        grid_spec=pltpu.PrefetchScalarGridSpec(
            num_scalar_prefetch=1,
            grid=(1,),
            in_specs=[pl.BlockSpec(memory_space=pl.ANY)] * n,
            out_specs=pl.BlockSpec(memory_space=pl.ANY),
            scratch_shapes=[pltpu.SemaphoreType.DMA((n,))],
        ),
        cost_estimate=pl.CostEstimate(
            flops=0, bytes_accessed=2 * sum(b.size * b.dtype.itemsize for b in blocks), transcendentals=0
        ),
    )(where, *blocks)


def axis_places(pos, sign):
    return jnp.stack([lax.rem(pos - k * sign + 8, 4) for k in range(4)]).astype(jnp.int32)


def gather_part(piece, order, pos, sign):
    first, second, last = order
    cols = piece.shape[1]
    rows = piece.shape[0]
    blocks = [piece] + [shift(piece, first, k) for k in (1, 2, 3)]
    ring = place(
        blocks, axis_places(pos[first], sign), (4, rows, cols), lambda i, w: w[i]
    )
    blocks = [ring] + [shift(ring, second, k) for k in (1, 2, 3)]
    natural = "yxz"
    firstmost = natural.index(second) < natural.index(first)
    if firstmost:
        at = lambda i, w: w[i]
    else:
        at = lambda i, w: (slice(None), w[i])
    plane = place(blocks, axis_places(pos[second], sign), (4, 4, rows, cols), at)
    groups = [plane]
    for _ in range(3):
        groups.append(shift(groups[-1], last, 1))
    return groups


def index_of(axis, q):
    return {"y": (q,), "x": (slice(None), q), "z": (slice(None), slice(None), q)}[axis]


def split_rows(rows):
    tiles = rows // 16
    a = -(-tiles // 3)
    b = -(-(tiles - a) // 2)
    return (a * 16, b * 16, rows - (a + b) * 16)


def proj_kernel(a0, a1, b, o0, o1, s0, s1):
    step = pl.program_id(0)

    @pl.when(step == 0)
    def _():
        s0[...] = jnp.zeros_like(s0)
        s1[...] = jnp.zeros_like(s1)

    s0[...] += jnp.dot(a0[...], b[...], preferred_element_type=F32)
    s1[...] += jnp.dot(a1[...], b[...], preferred_element_type=F32)

    @pl.when(step == pl.num_programs(0) - 1)
    def _():
        o0[...] = s0[...].astype(BF)
        o1[...] = s1[...].astype(BF)


def project(a0, a1, b):
    tok, depth = a0.shape
    cols = b.shape[1]
    kb = 1024
    return pl.pallas_call(
        proj_kernel,
        out_shape=[jax.ShapeDtypeStruct((tok, cols), BF)] * 2,
        grid=(depth // kb,),
        in_specs=[
            pl.BlockSpec((tok, kb), lambda i: (0, i)),
            pl.BlockSpec((tok, kb), lambda i: (0, i)),
            pl.BlockSpec((kb, cols), lambda i: (i, 0)),
        ],
        out_specs=[pl.BlockSpec((tok, cols), lambda i: (0, 0))] * 2,
        scratch_shapes=[pltpu.VMEM((tok, cols), F32)] * 2,
        cost_estimate=pl.CostEstimate(
            flops=4 * tok * depth * cols, bytes_accessed=4 * tok * depth + 2 * depth * cols, transcendentals=0
        ),
    )(a0, a1, b)


def partial_kernel(g0, g1, p0, p1, o):
    dims = (((0,), (0,)), ((), ()))
    o[...] = (
        lax.dot_general(g0[...], p0[...], dims, preferred_element_type=F32)
        + lax.dot_general(g1[...], p1[...], dims, preferred_element_type=F32)
    ).astype(BF)


def partials(g0, g1, p0, p1):
    tok, ffw = g0.shape
    cols = p0.shape[1]
    nb = 896
    return pl.pallas_call(
        partial_kernel,
        out_shape=jax.ShapeDtypeStruct((ffw, cols), BF),
        grid=(ffw // nb,),
        in_specs=[
            pl.BlockSpec((tok, nb), lambda i: (0, i)),
            pl.BlockSpec((tok, nb), lambda i: (0, i)),
            pl.BlockSpec((tok, cols), lambda i: (0, 0)),
            pl.BlockSpec((tok, cols), lambda i: (0, 0)),
        ],
        out_specs=pl.BlockSpec((nb, cols), lambda i: (i, 0)),
        cost_estimate=pl.CostEstimate(
            flops=4 * tok * ffw * cols, bytes_accessed=4 * tok * ffw + 2 * ffw * cols, transcendentals=0
        ),
    )(g0, g1, p0, p1)


def update_kernel(b, n, o):
    o[...] = (
        -galore_scale
        * lax.dot_general(b[...], n[...], (((1,), (1,)), ((), ())), preferred_element_type=F32)
    ).astype(BF)


def updates(basis, norm):
    rows, rank = basis.shape
    ffw = norm.shape[0]
    nb = 896
    return pl.pallas_call(
        update_kernel,
        out_shape=jax.ShapeDtypeStruct((rows, ffw), BF),
        grid=(ffw // nb,),
        in_specs=[
            pl.BlockSpec((rows, rank), lambda i: (0, 0)),
            pl.BlockSpec((nb, rank), lambda i: (i, 0)),
        ],
        out_specs=pl.BlockSpec((rows, nb), lambda i: (0, i)),
        cost_estimate=pl.CostEstimate(
            flops=2 * rows * ffw * rank, bytes_accessed=2 * (ffw * rank + rows * ffw), transcendentals=0
        ),
    )(basis, norm)


def local(activations, out_grads, basis, first_moment, second_moment):
    grp, fsdp = lax.axis_index("grp"), lax.axis_index("fsdp")
    core, low = grp % 2, grp // 2
    pos = {"y": fsdp // 8, "x": fsdp // 2 % 4, "z": (fsdp % 2) * 2 + low}
    sign = 1 - 2 * core
    rank = basis.shape[1]
    half = rank // 2
    ffw = out_grads.shape[1]
    shard = ffw // 64

    act_other = swap_core(activations)
    og_other = swap_core(out_grads)

    brows = basis.shape[0] // 2
    mine = lax.dynamic_slice(basis, (low * brows, core * half), (brows, half))
    blocks, codes, offset = [], [], 0
    for part, (size, order) in enumerate(zip(split_rows(brows), ORDERS)):
        groups = gather_part(mine[offset : offset + size], order, pos, sign)
        for k, group in enumerate(groups):
            blocks.append(group)
            codes.append((order[-1], part * 4 + k, offset, size))
        offset += size
    where = jnp.concatenate([axis_places(pos[order[-1]], sign) for order in ORDERS])

    def at_basis(i, w):
        axis, entry, start, size = codes[i]
        index = index_of(axis, w[entry])
        return index + (slice(None),) * (3 - len(index)) + (pl.ds(start, size),)

    full = place(blocks, where, (4, 4, 4, brows, half), at_basis).reshape(64 * brows, half)
    proj_own, proj_other = project(activations, act_other, full)
    partial = partials(out_grads, og_other, proj_own, proj_other).reshape(4, 4, 4, shard, half)

    sums, offset = [], 0
    for size, order in zip(split_rows(shard), ORDERS):
        third, second, first = order
        mine = partial[:, :, :, offset : offset + size]
        offset += size
        dim = "yxz".index(first)
        take = lambda k: lax.dynamic_index_in_dim(mine, lax.rem(pos[first] - k * sign + 8, 4), dim, keepdims=False)
        acc = take(1)
        for k in (2, 3, 4):
            acc = (shift(acc, first, 1).astype(F32) + take(k).astype(F32)).astype(BF)
        left = [a for a in "yxz" if a != first]
        for axis in (second, third):
            dim = left.index(axis)
            left.remove(axis)
            pick = lambda k: lax.dynamic_index_in_dim(
                acc, lax.rem(pos[axis] + k * sign + 8, 4), dim, keepdims=False
            )
            terms = [pick(0)] + [shift(pick(k), axis, k) for k in (1, 2, 3)]
            acc = sum(t.astype(F32) for t in terms).astype(BF)
        sums.append(acc)
    reduced = jnp.concatenate(sums, axis=0)

    def adam(first, second, red):
        new_first = beta_one * first + (1.0 - beta_one) * red
        new_second = beta_two * second + (1.0 - beta_two) * red * red
        return new_first, new_second

    at = (low * shard, core * half)
    new_first, new_second = adam(
        lax.dynamic_slice(first_moment, at, (shard, half)),
        lax.dynamic_slice(second_moment, at, (shard, half)),
        reduced.astype(F32),
    )
    corrected = new_first / (1.0 - beta_one**STEP)
    normalized = (corrected / (jnp.sqrt(new_second / (1.0 - beta_two**STEP)) + eps)).astype(BF)

    blocks, codes, offset = [], [], 0
    for part, (size, order) in enumerate(zip(split_rows(shard), ORDERS)):
        groups = gather_part(normalized[offset : offset + size], order, pos, sign)
        for k, group in enumerate(groups):
            blocks.append(group)
            codes.append((order[-1], part * 4 + k, offset, size, 12))
            blocks.append(swap_core(group))
            codes.append((order[-1], 14 + part * 4 + k, offset, size, 13))
        offset += size
    where = jnp.concatenate(
        [axis_places(pos[order[-1]], sign) for order in ORDERS]
        + [jnp.stack([core * half, half - core * half]).astype(jnp.int32)]
        + [axis_places(pos[order[-1]], -sign) for order in ORDERS]
    )

    def at_norm(i, w):
        axis, entry, start, size, column = codes[i]
        index = index_of(axis, w[entry])
        return index + (slice(None),) * (3 - len(index)) + (
            pl.ds(start, size),
            pl.ds(pl.multiple_of(w[column], half), half),
        )

    norm = place(blocks, where, (4, 4, 4, shard, rank), at_norm).reshape(ffw, rank)
    update = updates(basis, norm)

    other = swap_core(reduced)
    row = jnp.where(core == 0, jnp.concatenate([reduced, other], 1), jnp.concatenate([other, reduced], 1))
    other = swap_low(row)
    rows = jnp.where(low == 0, jnp.concatenate([row, other], 0), jnp.concatenate([other, row], 0))
    out_first, out_second = adam(first_moment, second_moment, rows.astype(F32))
    return (update, out_first, out_second)


def solution(mesh):
    in_specs = (
        P(("grp", "fsdp"), None),
        P(("grp", "fsdp"), None),
        P("fsdp", None),
        P("fsdp", None),
        P("fsdp", None),
    )
    out_specs = (P("fsdp", None), P("fsdp", None), P("fsdp", None))
    return jax.shard_map(local, mesh=mesh, in_specs=in_specs, out_specs=out_specs, check_vma=False)
```

```python
import itertools

import jax
import jax.numpy as jnp
from jax import lax
from jax.experimental import pallas as pl
from jax.experimental.pallas import tpu as pltpu
from jax.sharding import Mesh
from jax.sharding import PartitionSpec as P

STEP = 10


beta_one = 0.9
beta_two = 0.99
eps = 1e-08
galore_scale = 4.0

BF = jnp.bfloat16
F32 = jnp.float32
AXES = ("zl", "c", "y1", "y0", "x1", "x0", "zh")
FSDP = ("y1", "y0", "x1", "x0", "zh")
ORDERS = ("xyz", "yzx", "zxy")


def flat(co):
    return ((co["z"] % 2) * 2 + co["c"]) * 32 + (co["y"] * 4 + co["x"]) * 2 + co["z"] // 2


def permute(arr, move):
    pairs = []
    for c in range(2):
        for y in range(4):
            for x in range(4):
                for z in range(4):
                    co = {"c": c, "y": y, "x": x, "z": z}
                    pairs.append((flat(co), flat(move(dict(co)))))
    return lax.ppermute(arr, AXES, pairs)


def swap(arr, axis, late=0):
    def move(co):
        co[axis] ^= 3 if co["c"] != late else 1
        return co

    return permute(arr, move)


def swap_core(arr):
    def move(co):
        co["c"] ^= 1
        return co

    return permute(arr, move)


def swap_low(arr):
    def move(co):
        co["z"] ^= 1
        return co

    return permute(arr, move)


def split_rows(rows):
    tiles = rows // 16
    a = -(-tiles // 3)
    b = -(-(tiles - a) // 2)
    return (a * 16, b * 16, rows - (a + b) * 16)


def starts(sizes):
    return (0, sizes[0], sizes[0] + sizes[1])


def join(arrays, gots, extra):
    n = len(arrays)
    *both, extra = lax.optimization_barrier((*arrays, *gots, extra))
    return [jnp.stack(pair) for pair in zip(both[:n], both[n:])], extra


def gather(piece, extra):
    for axis in "zxy":
        (piece,), extra = join([piece], [swap(piece, axis, late=1)], extra)
    sizes = split_rows(piece.shape[3])
    parts = [piece[:, :, :, begin : begin + size] for size, begin in zip(sizes, starts(sizes))]
    for stage in (2, 1):
        gots = [swap(part, order[stage]) for order, part in zip(ORDERS, parts)]
        parts, extra = join(parts, gots, extra)
    return [(part, swap(part, order[0])) for order, part in zip(ORDERS, parts)], extra


def bits(place, core):
    high = place // 2
    low = lax.bitwise_xor(place % 2, high)
    return low + core * (high - low), high + core * (low - high)


def place_of(u, v, core):
    high, low = v + core * (u - v), u + core * (v - u)
    return high * 2 + lax.bitwise_xor(high, low)


def load_block(parts, y, x, pos_ref, core):
    y, x = bits(lax.bitwise_xor(pos_ref[0], y), core), bits(lax.bitwise_xor(pos_ref[1], x), core)
    rows = []
    for place in range(4):
        z = bits(lax.bitwise_xor(pos_ref[2], place), core)
        by = {"y": y, "x": x, "z": z}
        for order, part in zip(ORDERS, parts):
            rows.append(part[tuple(by[a][0] for a in order) + (y[1], x[1], z[1])])
    return jnp.concatenate(rows, axis=0)


def part_scratch(sizes, cols):
    return [pltpu.VMEM((2, 2, 2, 2, 2, 2, size, cols), BF) for size in sizes]


def load_copies(arrays, parts, sem):
    return [
        pltpu.make_async_copy(arrays[2 * i + u], part.at[u], sem.at[2 * i + u])
        for i, part in enumerate(parts)
        for u in range(2)
    ]


def project(a0, a1, parts, pos):
    tok, depth = a0.shape
    arrays = [a for pair in parts for a in pair]
    cols = arrays[0].shape[-1]
    kb = 1024
    steps = depth // kb

    def kernel(pos_ref, *refs):
        srcs, (a0_ref, a1_ref, o0, o1, s0, s1), scratch, sem = refs[:6], refs[6:12], refs[12:15], refs[15]
        step = pl.program_id(0)

        @pl.when(step == 0)
        def _():
            copies = load_copies(srcs, scratch, sem)
            for copy in copies:
                copy.start()
            s0[...] = jnp.zeros_like(s0)
            s1[...] = jnp.zeros_like(s1)
            for copy in copies:
                copy.wait()

        y, x = step // 2, step % 2 * 2
        b = jnp.concatenate([load_block(scratch, y, x + k, pos_ref, pos_ref[3]) for k in range(2)], axis=0)
        s0[...] += jnp.dot(a0_ref[...], b, preferred_element_type=F32)
        s1[...] += jnp.dot(a1_ref[...], b, preferred_element_type=F32)

        @pl.when(step == steps - 1)
        def _():
            o0[...] = s0[...].astype(BF)
            o1[...] = s1[...].astype(BF)

    return pl.pallas_call(
        kernel,
        out_shape=[jax.ShapeDtypeStruct((tok, cols), BF)] * 2,
        grid_spec=pltpu.PrefetchScalarGridSpec(
            num_scalar_prefetch=1,
            grid=(steps,),
            in_specs=[pl.BlockSpec(memory_space=pl.ANY)] * 6
            + [pl.BlockSpec((tok, kb), lambda i, w: (0, i))] * 2,
            out_specs=[pl.BlockSpec((tok, cols), lambda i, w: (0, 0))] * 2,
            scratch_shapes=[pltpu.VMEM((tok, cols), F32)] * 2
            + part_scratch([p[0].shape[-2] for p in parts], cols)
            + [pltpu.SemaphoreType.DMA((6,))],
        ),
        compiler_params=pltpu.CompilerParams(vmem_limit_bytes=32 * 2**20),
        cost_estimate=pl.CostEstimate(
            flops=4 * tok * depth * cols, bytes_accessed=4 * tok * depth + 2 * depth * cols, transcendentals=0
        ),
    )(pos, *arrays, a0, a1)


def partials(g0, g1, p0, p1, pos):
    tok, ffw = g0.shape
    cols = p0.shape[1]
    nb = ffw // 16
    rows = nb // 4
    sizes = split_rows(rows)

    def block(i, w):
        y, x = place_of(i // 8, i // 2 % 2, w[3]), place_of(i // 4 % 2, i % 2, w[3])
        return 0, lax.bitwise_xor(w[0], y) * 4 + lax.bitwise_xor(w[1], x)

    def kernel(pos_ref, g0_ref, g1_ref, p0_ref, p1_ref, *refs):
        outs, scratch = refs[:6], refs[6]
        dims = (((0,), (0,)), ((), ()))
        i = pl.program_id(0)
        u = {"y": i // 8, "x": i // 4 % 2}
        vy, vx = i // 2 % 2, i % 2
        scratch[...] = (
            (
                lax.dot_general(g0_ref[...], p0_ref[...], dims, preferred_element_type=F32)
                + lax.dot_general(g1_ref[...], p1_ref[...], dims, preferred_element_type=F32)
            )
            .astype(BF)
            .reshape(4, rows, cols)
        )
        for part, (order, size, begin) in enumerate(zip(ORDERS, sizes, starts(sizes))):
            for first in range(2):
                ref = outs[2 * part + first]

                def store(uz, ref=ref, order=order, size=size, begin=begin):
                    at = {**u, "z": uz}
                    for vz in range(2):
                        z = lax.bitwise_xor(pos_ref[2], place_of(uz, vz, pos_ref[3]))
                        ref[at[order[1]], at[order[2]], vy, vx, vz] = scratch[z, pl.ds(begin, size)]

                if order[0] == "z":
                    store(first)
                else:

                    @pl.when(u[order[0]] == first)
                    def _(store=store):
                        store(0)
                        store(1)

    shapes = [(2, 2, 2, 2, 2, size, cols) for size in sizes for _ in range(2)]
    return pl.pallas_call(
        kernel,
        out_shape=[jax.ShapeDtypeStruct(s, BF) for s in shapes],
        grid_spec=pltpu.PrefetchScalarGridSpec(
            num_scalar_prefetch=1,
            grid=(16,),
            in_specs=[
                pl.BlockSpec((tok, nb), block),
                pl.BlockSpec((tok, nb), block),
                pl.BlockSpec((tok, cols), lambda i, w: (0, 0)),
                pl.BlockSpec((tok, cols), lambda i, w: (0, 0)),
            ],
            out_specs=[pl.BlockSpec(s, lambda i, w: (0,) * 7) for s in shapes],
            scratch_shapes=[pltpu.VMEM((4, rows, cols), BF)],
        ),
        compiler_params=pltpu.CompilerParams(vmem_limit_bytes=40 * 2**20),
        cost_estimate=pl.CostEstimate(
            flops=4 * tok * ffw * cols, bytes_accessed=4 * tok * ffw + 2 * ffw * cols, transcendentals=0
        ),
    )(pos, g0, g1, p0, p1)


def updates(basis, own, other, pos):
    rows, rank = basis.shape
    arrays = [a for parts in (own, other) for pair in parts for a in pair]
    half = arrays[0].shape[-1]
    sizes = [parts[0].shape[-2] for parts in own]
    nb = 4 * sum(sizes)
    ffw = 16 * nb

    def kernel(pos_ref, *refs):
        srcs, (b_ref, o), s0, s1, sem = refs[:12], refs[12:14], refs[14:17], refs[17:20], refs[20]
        step = pl.program_id(0)

        @pl.when(step == 0)
        def _():
            copies = load_copies(srcs[:6], s0, sem.at[0]) + load_copies(srcs[6:], s1, sem.at[1])
            for copy in copies:
                copy.start()
            for copy in copies:
                copy.wait()

        dims = (((1,), (1,)), ((), ()))
        core = pos_ref[3]
        y, x = step // 4, step % 4
        total = lax.dot_general(
            b_ref[core], load_block(s0, y, x, pos_ref, core), dims, preferred_element_type=F32
        ) + lax.dot_general(
            b_ref[1 - core], load_block(s1, y, x, pos_ref, 1 - core), dims, preferred_element_type=F32
        )
        o[...] = (-galore_scale * total).astype(BF)

    halves = jnp.stack([basis[:, :half], basis[:, half:]])
    return pl.pallas_call(
        kernel,
        out_shape=jax.ShapeDtypeStruct((rows, ffw), BF),
        grid_spec=pltpu.PrefetchScalarGridSpec(
            num_scalar_prefetch=1,
            grid=(16,),
            in_specs=[pl.BlockSpec(memory_space=pl.ANY)] * 12
            + [pl.BlockSpec((2, rows, half), lambda i, w: (0, 0, 0))],
            out_specs=pl.BlockSpec((rows, nb), lambda i, w: (0, i)),
            scratch_shapes=part_scratch(sizes, half) * 2 + [pltpu.SemaphoreType.DMA((2, 6))],
        ),
        compiler_params=pltpu.CompilerParams(vmem_limit_bytes=40 * 2**20),
        cost_estimate=pl.CostEstimate(
            flops=2 * rows * ffw * rank, bytes_accessed=2 * (ffw * rank + rows * ffw), transcendentals=0
        ),
    )(pos, *arrays, halves)


def add(a, b):
    return (a.astype(F32) + b.astype(F32)).astype(BF)


def local(activations, out_grads, basis, first_moment, second_moment):
    core, zl = lax.axis_index("c"), lax.axis_index("zl")
    places = [lax.axis_index(a + "1") * 2 + lax.axis_index(a + "0") for a in "yx"] + [lax.axis_index("zh") * 2 + zl]
    pos = jnp.stack(places + [core]).astype(jnp.int32)
    rank = basis.shape[1]
    half = rank // 2
    shard = out_grads.shape[1] // 64
    brows = basis.shape[0] // 2

    act_other = swap_core(activations)
    g_other = swap_core(out_grads)

    parts, zl = gather(lax.dynamic_slice(basis, (zl * brows, core * half), (brows, half)), zl)
    proj_own, proj_other = project(activations, act_other, parts, pos)
    sums = partials(out_grads, g_other, proj_own, proj_other, pos)

    keeps, sends = sums[0::2], sums[1::2]
    for stage in range(3):
        gots = [swap(send, order[stage]) for order, send in zip(ORDERS, sends)]
        sends = [add(keep[1], got[1]) for keep, got in zip(keeps, gots)]
        keeps = [add(keep[0], got[0]) for keep, got in zip(keeps, gots)]
    keep, send = jnp.concatenate(keeps, axis=-2), jnp.concatenate(sends, axis=-2)
    for axis in "yx":
        got = swap(send, axis, late=1)
        send = add(keep[1], got[1])
        keep = add(keep[0], got[0])
    reduced = add(keep, swap(send, "z", late=1))

    def adam(first, second, red):
        new_first = beta_one * first + (1.0 - beta_one) * red
        new_second = beta_two * second + (1.0 - beta_two) * red * red
        return new_first, new_second

    at = (zl * shard, core * half)
    new_first, new_second = adam(
        lax.dynamic_slice(first_moment, at, (shard, half)),
        lax.dynamic_slice(second_moment, at, (shard, half)),
        reduced.astype(F32),
    )
    corrected = new_first / (1.0 - beta_one**STEP)
    normalized = (corrected / (jnp.sqrt(new_second / (1.0 - beta_two**STEP)) + eps)).astype(BF)

    other = swap_core(reduced)
    row = jnp.where(core == 0, jnp.concatenate([reduced, other], 1), jnp.concatenate([other, reduced], 1))
    other = swap_low(row)
    rows = jnp.where(zl == 0, jnp.concatenate([row, other], 0), jnp.concatenate([other, row], 0))

    own, rows = gather(normalized, rows)
    other = [(swap_core(a), swap_core(b)) for a, b in own]
    update = updates(basis, own, other, pos)
    out_first, out_second = adam(first_moment, second_moment, rows.astype(F32))
    return (update, out_first, out_second)


def solution(mesh):
    chips = Mesh(mesh.devices.reshape(2, 2, 2, 2, 2, 2, 2), AXES)
    in_specs = (P(AXES, None), P(AXES, None), P(FSDP, None), P(FSDP, None), P(FSDP, None))
    out_specs = (P(FSDP, None), P(FSDP, None), P(FSDP, None))
    return jax.shard_map(local, mesh=chips, in_specs=in_specs, out_specs=out_specs, check_vma=False)
```

```python
import itertools

import jax
import jax.numpy as jnp
from jax import lax
from jax.experimental import pallas as pl
from jax.experimental.pallas import tpu as pltpu
from jax.sharding import Mesh
from jax.sharding import PartitionSpec as P

STEP = 10


beta_one = 0.9
beta_two = 0.99
eps = 1e-08
galore_scale = 4.0

BF = jnp.bfloat16
F32 = jnp.float32
AXES = ("zl", "c", "y1", "y0", "x1", "x0", "zh")
FSDP = ("y1", "y0", "x1", "x0", "zh")
ORDERS = ("xyz", "yzx", "zxy")


def flat(co):
    return ((co["z"] % 2) * 2 + co["c"]) * 32 + (co["y"] * 4 + co["x"]) * 2 + co["z"] // 2


def permute(arr, move):
    pairs = []
    for c in range(2):
        for y in range(4):
            for x in range(4):
                for z in range(4):
                    co = {"c": c, "y": y, "x": x, "z": z}
                    pairs.append((flat(co), flat(move(dict(co)))))
    return lax.ppermute(arr, AXES, pairs)


def swap(arr, axis, late=0):
    def move(co):
        co[axis] ^= 3 if co["c"] != late else 1
        return co

    return permute(arr, move)


def swap_core(arr):
    def move(co):
        co["c"] ^= 1
        return co

    return permute(arr, move)


def swap_low(arr):
    def move(co):
        co["z"] ^= 1
        return co

    return permute(arr, move)


PARTS = ((0, 3), (3, 6), (6, 8))


def join(arrays, gots, *extra):
    n = len(arrays)
    both = lax.optimization_barrier((*arrays, *gots, *extra))
    return [jnp.stack(pair) for pair in zip(both[:n], both[n : 2 * n])], *both[2 * n :]


def gather(piece, beside):
    tied = ()
    for axis in "zxy"[piece.ndim - 2 :]:
        got = swap(piece, axis, late=1)
        if beside:
            tied = beside[0](*tied)
        (piece,), *tied = join([piece], [got], *tied)
        beside = beside[1:]
    piece = piece.reshape(8, *piece.shape[3:])
    parts = [piece[begin:end] for begin, end in PARTS]
    for stage in (2, 1):
        gots = [swap(part, order[stage]) for order, part in zip(ORDERS, parts)]
        if beside:
            tied = beside[0](*tied)
        parts, *tied = join(parts, gots, *tied)
        beside = beside[1:]
    return parts, [swap(part, order[0]) for order, part in zip(ORDERS, parts)], tied


def bits(place, core):
    high = place // 2
    low = lax.bitwise_xor(place % 2, high)
    return low + core * (high - low), high + core * (low - high)


def place_of(u, v, core):
    high, low = v + core * (u - v), u + core * (v - u)
    return high * 2 + lax.bitwise_xor(high, low)


def chips():
    for uy, ux, vy, vx in itertools.product(range(2), repeat=4):
        yield [({"y": uy, "x": ux, "z": uz}, vy * 4 + vx * 2 + vz) for uz in range(2) for vz in range(2)]


def absolute(u, v, axis, pos_ref, core):
    j = "yxz".index(axis)
    return lax.bitwise_xor(pos_ref[j], place_of(u[axis], v // (4, 2, 1)[j] % 2, core))


def part_of(v):
    return next((i, v - begin) for i, (begin, end) in enumerate(PARTS) if v < end)


SMEM = pl.BlockSpec(memory_space=pltpu.SMEM)
VMEM = pl.BlockSpec(memory_space=pltpu.VMEM)
HBM = pl.BlockSpec(memory_space=pltpu.HBM)


def place(whole, arrays, which, pos, core):
    rows, cols = arrays[0].shape[-2:]
    size = 64 * rows * cols

    def kernel(pos_ref, core_ref, *refs):
        out = refs[-1]
        for run in chips():
            for u, v in run:
                part, w = part_of(v)
                first, second, third = (u[a] for a in ORDERS[part])
                if first == which:
                    y, x, z = (absolute(u, v, a, pos_ref, core_ref[0]) for a in "yxz")
                    out[(y * 4 + x) * 4 + z] = refs[part][second, third, w]

    return pl.pallas_call(
        kernel,
        out_shape=jax.ShapeDtypeStruct((64, rows, cols), BF),
        in_specs=[SMEM] * 2 + [VMEM] * (3 if whole is None else 4),
        out_specs=VMEM,
        input_output_aliases={} if whole is None else {5: 0},
        compiler_params=pltpu.CompilerParams(vmem_limit_bytes=8 * 2**20),
        cost_estimate=pl.CostEstimate(flops=0, bytes_accessed=2 * size, transcendentals=0),
    )(pos, core, *arrays, *(() if whole is None else (whole,)))


def load(*arrays):
    n, cuts = len(arrays), 4

    def kernel(*refs):
        sem = refs[-1]
        copies = []
        for src, dst in zip(refs[:n], refs[n:]):
            rows = src.shape[0] // cuts
            for i in range(cuts):
                at = pl.ds(i * rows, rows)
                copies.append(pltpu.make_async_copy(src.at[at], dst.at[at], sem.at[len(copies)]))
        for copy in copies:
            copy.start()
        for copy in copies:
            copy.wait()

    return pl.pallas_call(
        kernel,
        out_shape=[jax.ShapeDtypeStruct(a.shape, a.dtype) for a in arrays],
        in_specs=[HBM] * n,
        out_specs=[VMEM] * n,
        scratch_shapes=[pltpu.SemaphoreType.DMA((n * cuts,))],
        compiler_params=pltpu.CompilerParams(vmem_limit_bytes=8 * 2**20),
        cost_estimate=pl.CostEstimate(flops=0, bytes_accessed=sum(2 * a.size for a in arrays), transcendentals=0),
    )(*arrays)


def project(a0, a1, whole):
    tok, depth = a0.shape
    cols = whole.shape[2]

    def kernel(a0_ref, a1_ref, b_ref, o0, o1):
        a = jnp.concatenate([a0_ref[...], a1_ref[...]])
        out = jnp.dot(a, b_ref[...].reshape(depth, cols), preferred_element_type=F32).astype(BF)
        o0[...] = out[:tok]
        o1[...] = out[tok:]

    return pl.pallas_call(
        kernel,
        out_shape=[jax.ShapeDtypeStruct((tok, cols), BF)] * 2,
        in_specs=[VMEM] * 3,
        out_specs=[VMEM] * 2,
        compiler_params=pltpu.CompilerParams(vmem_limit_bytes=8 * 2**20),
        cost_estimate=pl.CostEstimate(
            flops=4 * tok * depth * cols, bytes_accessed=4 * tok * depth + 2 * depth * cols, transcendentals=0
        ),
    )(a0, a1, whole)


def partials(g0, g1, p0, p1, pos, keeps=None):
    tok, ffw = g0.shape
    cols = p0.shape[1]
    nb = ffw // 16
    rows = nb // 4

    def sent(u, v):
        return u[ORDERS[part_of(v)[0]][0]]

    runs = [run for run in chips() if any(sent(u, v) for u, v in run) == (keeps is None)]

    def kernel(pos_ref, g0_ref, g1_ref, p0_ref, p1_ref, *refs):
        dims = (((0,), (0,)), ((), ()))
        columns = []
        for run in runs:
            y, x = (absolute(*run[0], a, pos_ref, pos_ref[3]) for a in "yx")
            columns.append(pl.ds(pl.multiple_of((y * 4 + x) * nb, nb), nb))
        if keeps is None:
            *send_refs, keep_x, keep_y, keep_z, scratch = refs
            keep_refs = keep_x, keep_y, keep_z
        else:
            *_, keep_x, keep_y, keep_z, scratch, held, sem = refs
            keep_refs = keep_x, keep_y, keep_z
            copies = [
                [pltpu.make_async_copy(g.at[:, at], held.at[i, j], sem.at[i, j]) for j, g in enumerate((g0_ref, g1_ref))]
                for i, at in enumerate(columns)
            ]
            for copy in itertools.chain(*copies):
                copy.start()
        for i, (run, at) in enumerate(zip(runs, columns)):
            if keeps is None:
                terms = g0_ref[:, at], g1_ref[:, at]
            else:
                for copy in copies[i]:
                    copy.wait()
                terms = held[i, 0], held[i, 1]
            scratch[i % 2] = (
                (
                    lax.dot_general(terms[0], p0_ref[...], dims, preferred_element_type=F32)
                    + lax.dot_general(terms[1], p1_ref[...], dims, preferred_element_type=F32)
                )
                .astype(BF)
                .reshape(4, rows, cols)
            )
            for u, v in run:
                part, w = part_of(v)
                _, second, third = (u[a] for a in ORDERS[part])
                outs = send_refs if sent(u, v) else keep_refs
                outs[part][second, third, w] = scratch[i % 2, absolute(u, v, "z", pos_ref, pos_ref[3])]

    shapes = [(2, 2, end - begin, rows, cols) for begin, end in PARTS] * (2 if keeps is None else 1)
    share = len(runs) / 16
    return pl.pallas_call(
        kernel,
        out_shape=[jax.ShapeDtypeStruct(s, BF) for s in shapes],
        in_specs=[SMEM] + ([VMEM] * 4 if keeps is None else [HBM] * 2 + [VMEM] * 5),
        out_specs=[VMEM] * len(shapes),
        input_output_aliases={} if keeps is None else {5: 0, 6: 1, 7: 2},
        scratch_shapes=[pltpu.VMEM((2, 4, rows, cols), BF)]
        + ([] if keeps is None else [pltpu.VMEM((len(runs), 2, tok, nb), BF), pltpu.SemaphoreType.DMA((len(runs), 2))]),
        compiler_params=pltpu.CompilerParams(vmem_limit_bytes=(6 if keeps is None else 12) * 2**20),
        cost_estimate=pl.CostEstimate(
            flops=int(4 * tok * ffw * cols * share),
            bytes_accessed=int((4 * tok * ffw + 2 * ffw * cols) * share),
            transcendentals=0,
        ),
    )(pos, g0, g1, p0, p1, *(keeps or ()))


def updates(basis, own, other, core):
    rows, rank = basis.shape
    shard, half = own.shape[1:]
    nb = 4 * shard
    ffw = 16 * nb

    def kernel(core_ref, own_ref, other_ref, b_ref, out, stage, sem):
        dims = (((1,), (1,)), ((), ()))
        core = core_ref[0]
        copies = []
        for i in range(16):
            at = pl.ds(i * nb, nb)
            total = lax.dot_general(
                b_ref[core], own_ref[4 * i : 4 * i + 4].reshape(nb, half), dims, preferred_element_type=F32
            ) + lax.dot_general(
                b_ref[1 - core], other_ref[4 * i : 4 * i + 4].reshape(nb, half), dims, preferred_element_type=F32
            )
            stage[:, at] = (-galore_scale * total).astype(BF)
            copies.append(pltpu.make_async_copy(stage.at[:, at], out.at[:, at], sem.at[i]))
            copies[-1].start()
        for copy in copies:
            copy.wait()

    halves = jnp.stack([basis[:, :half], basis[:, half:]])
    return pl.pallas_call(
        kernel,
        out_shape=jax.ShapeDtypeStruct((rows, ffw), BF),
        in_specs=[SMEM] + [VMEM] * 3,
        out_specs=pl.BlockSpec(memory_space=pl.ANY),
        scratch_shapes=[pltpu.VMEM((rows, ffw), BF), pltpu.SemaphoreType.DMA((16,))],
        compiler_params=pltpu.CompilerParams(vmem_limit_bytes=12 * 2**20),
        cost_estimate=pl.CostEstimate(
            flops=2 * rows * ffw * rank, bytes_accessed=2 * (ffw * rank + rows * ffw), transcendentals=0
        ),
    )(core, own, other, halves)


def add(a, b):
    return (a.astype(F32) + b.astype(F32)).astype(BF)


def local(activations, out_grads, basis, first_moment, second_moment):
    core, zl = lax.axis_index("c"), lax.axis_index("zl")
    places = [lax.axis_index(a + "1") * 2 + lax.axis_index(a + "0") for a in "yx"] + [lax.axis_index("zh") * 2 + zl]
    pos = jnp.stack(places + [core]).astype(jnp.int32)
    rank = basis.shape[1]
    half = rank // 2
    shard = out_grads.shape[1] // 64
    brows = basis.shape[0] // 2

    act_other = swap_core(activations)
    g_other = swap_core(out_grads)

    mine, theirs = pos[3:], 1 - pos[3:]
    swapped = [lambda: ()] * 4 + [lambda: (act_other, g_other)]
    near, far, (act_other, g_other) = gather(
        lax.dynamic_slice(basis, (zl * brows, core * half), (brows, half)), swapped
    )
    whole = place(place(None, near, 0, pos, mine), far, 1, pos, mine)
    near_acts = load(activations, act_other)
    near_gs = load(out_grads, g_other)
    terms = (*project(*near_acts, whole), pos)
    *sends, keep_x, keep_y, keep_z = partials(*near_gs, *terms)
    keeps = partials(out_grads, g_other, *terms, [keep_x, keep_y, keep_z])

    at = (zl * shard, core * half)
    moments = [lax.dynamic_slice(m, at, (shard, half)) for m in (first_moment, second_moment)]
    moments = lax.optimization_barrier((jnp.stack(moments), *sends))[0]

    for stage in range(3):
        gots = [swap(send, order[stage]) for order, send in zip(ORDERS, sends)]
        if stage == 0:
            *gots, theirs_moments = lax.optimization_barrier((*gots, swap(moments, "z", late=1)))
        if stage < 2:
            sends = [add(keep[1], got[1]) for keep, got in zip(keeps, gots)]
            keeps = [add(keep[0], got[0]) for keep, got in zip(keeps, gots)]
        else:
            keeps = [add(keep, got) for keep, got in zip(keeps, gots)]
    keep = jnp.concatenate(keeps).reshape(2, 2, 2, shard, half)
    keep, send = keep[0], keep[1]
    for axis in "yx":
        got = swap(send, axis, late=1)
        send = add(keep[1], got[1])
        keep = add(keep[0], got[0])
    keep = jnp.stack([keep, send])
    blocks = add(keep, swap(keep, "z", late=1)[::-1])
    reduced = blocks[0]

    def adam(first, second, red):
        new_first = beta_one * first + (1.0 - beta_one) * red
        new_second = beta_two * second + (1.0 - beta_two) * red * red
        return new_first, new_second

    new_first, new_second = adam(*jnp.stack([moments, theirs_moments], axis=1), blocks.astype(F32))
    corrected = new_first / (1.0 - beta_one**STEP)
    normalized = (corrected / (jnp.sqrt(new_second / (1.0 - beta_two**STEP)) + eps)).astype(BF)

    def columns():
        other = swap_core(reduced)
        both = jnp.concatenate([reduced, other], 1), jnp.concatenate([other, reduced], 1)
        return (jnp.where(core == 0, *both),)

    def rows(own):
        other = swap_low(own)
        return (jnp.where(zl == 0, jnp.concatenate([own, other]), jnp.concatenate([other, own])),)

    near, far, (rows,) = gather(normalized, [columns, rows])
    own = place(None, near, 0, pos, mine)
    near = lax.optimization_barrier((*near, own))[:3]
    other = place(None, [swap_core(a) for a in near], 0, pos, theirs)
    update = updates(
        basis, place(own, far, 1, pos, mine), place(other, [swap_core(a) for a in far], 1, pos, theirs), mine
    )
    out_first, out_second = adam(first_moment, second_moment, rows.astype(F32))
    return (update, out_first, out_second)


def solution(mesh):
    chips = Mesh(mesh.devices.reshape(2, 2, 2, 2, 2, 2, 2), AXES)
    in_specs = (P(AXES, None), P(AXES, None), P(FSDP, None), P(FSDP, None), P(FSDP, None))
    out_specs = (P(FSDP, None), P(FSDP, None), P(FSDP, None))
    return jax.shard_map(local, mesh=chips, in_specs=in_specs, out_specs=out_specs, check_vma=False)
```

```python
import itertools

import jax
import jax.numpy as jnp
from jax import lax
from jax.experimental import pallas as pl
from jax.experimental.pallas import tpu as pltpu
from jax.sharding import Mesh
from jax.sharding import PartitionSpec as P

STEP = 10


beta_one = 0.9
beta_two = 0.99
eps = 1e-08
galore_scale = 4.0

BF = jnp.bfloat16
F32 = jnp.float32
AXES = ("zl", "c", "y1", "y0", "x1", "x0", "zh")
FSDP = ("y1", "y0", "x1", "x0", "zh")
ORDERS = ("xyz", "yzx", "zxy")


def flat(co):
    return ((co["z"] % 2) * 2 + co["c"]) * 32 + (co["y"] * 4 + co["x"]) * 2 + co["z"] // 2


def permute(arr, move):
    pairs = []
    for c in range(2):
        for y in range(4):
            for x in range(4):
                for z in range(4):
                    co = {"c": c, "y": y, "x": x, "z": z}
                    pairs.append((flat(co), flat(move(dict(co)))))
    return lax.ppermute(arr, AXES, pairs)


def swap(arr, axes, late=0):
    def move(co):
        for axis in axes:
            co[axis] ^= 3 if co["c"] != late else 1
        return co

    return permute(arr, move)


def swap_core(arr):
    def move(co):
        co["c"] ^= 1
        return co

    return permute(arr, move)


def swap_low(arr):
    def move(co):
        co["z"] ^= 1
        return co

    return permute(arr, move)


PARTS = ((0, 3), (3, 6), (6, 8))


def join(arrays, gots, *extra):
    n = len(arrays)
    both = lax.optimization_barrier((*arrays, *gots, *extra))
    return [jnp.stack(pair) for pair in zip(both[:n], both[n : 2 * n])], *both[2 * n :]


def gather(piece, beside):
    tied = ()
    if piece.ndim == 2:
        ((piece,),) = join([piece], [swap(piece, "z", late=1)])
    gots = [swap(piece, axes, late=1) for axes in ("x", "y", "xy")]
    if beside:
        tied = beside[0](*tied)
    blocks = lax.optimization_barrier((piece, *gots, *tied))
    tied, beside = blocks[4:], beside[1:]
    piece = jnp.concatenate(blocks[:4])
    parts = [piece[begin:end] for begin, end in PARTS]
    for stage in (2, 1):
        gots = [swap(part, order[stage]) for order, part in zip(ORDERS, parts)]
        if beside:
            tied = beside[0](*tied)
        parts, *tied = join(parts, gots, *tied)
        beside = beside[1:]
    return parts, [swap(part, order[0]) for order, part in zip(ORDERS, parts)], tied


def bits(place, core):
    high = place // 2
    low = lax.bitwise_xor(place % 2, high)
    return low + core * (high - low), high + core * (low - high)


def place_of(u, v, core):
    high, low = v + core * (u - v), u + core * (v - u)
    return high * 2 + lax.bitwise_xor(high, low)


def chips():
    for uy, ux, vy, vx in itertools.product(range(2), repeat=4):
        yield [({"y": uy, "x": ux, "z": uz}, vy * 4 + vx * 2 + vz) for uz in range(2) for vz in range(2)]


def absolute(u, v, axis, pos_ref, core):
    j = "yxz".index(axis)
    return lax.bitwise_xor(pos_ref[j], place_of(u[axis], v // (4, 2, 1)[j] % 2, core))


def part_of(v):
    return next((i, v - begin) for i, (begin, end) in enumerate(PARTS) if v < end)


SMEM = pl.BlockSpec(memory_space=pltpu.SMEM)
VMEM = pl.BlockSpec(memory_space=pltpu.VMEM)
HBM = pl.BlockSpec(memory_space=pltpu.HBM)


def place(whole, arrays, which, pos, core):
    rows, cols = arrays[0].shape[-2:]
    size = 64 * rows * cols

    def kernel(pos_ref, core_ref, *refs):
        out = refs[-1]
        for run in chips():
            for u, v in run:
                part, w = part_of(v)
                first, second, third = (u[a] for a in ORDERS[part])
                if first == which:
                    y, x, z = (absolute(u, v, a, pos_ref, core_ref[0]) for a in "yxz")
                    out[(y * 4 + x) * 4 + z] = refs[part][second, third, w]

    return pl.pallas_call(
        kernel,
        out_shape=jax.ShapeDtypeStruct((64, rows, cols), BF),
        in_specs=[SMEM] * 2 + [VMEM] * (3 if whole is None else 4),
        out_specs=VMEM,
        input_output_aliases={} if whole is None else {5: 0},
        compiler_params=pltpu.CompilerParams(vmem_limit_bytes=8 * 2**20),
        cost_estimate=pl.CostEstimate(flops=0, bytes_accessed=2 * size, transcendentals=0),
    )(pos, core, *arrays, *(() if whole is None else (whole,)))


def load(*arrays):
    n, cuts = len(arrays), 4

    def kernel(*refs):
        sem = refs[-1]
        copies = []
        for src, dst in zip(refs[:n], refs[n:]):
            rows = src.shape[0] // cuts
            for i in range(cuts):
                at = pl.ds(i * rows, rows)
                copies.append(pltpu.make_async_copy(src.at[at], dst.at[at], sem.at[len(copies)]))
        for copy in copies:
            copy.start()
        for copy in copies:
            copy.wait()

    return pl.pallas_call(
        kernel,
        out_shape=[jax.ShapeDtypeStruct(a.shape, a.dtype) for a in arrays],
        in_specs=[HBM] * n,
        out_specs=[VMEM] * n,
        scratch_shapes=[pltpu.SemaphoreType.DMA((n * cuts,))],
        compiler_params=pltpu.CompilerParams(vmem_limit_bytes=8 * 2**20),
        cost_estimate=pl.CostEstimate(flops=0, bytes_accessed=sum(2 * a.size for a in arrays), transcendentals=0),
    )(*arrays)


def project(a0, a1, whole):
    tok, depth = a0.shape
    cols = whole.shape[2]

    def kernel(a0_ref, a1_ref, b_ref, o0, o1):
        a = jnp.concatenate([a0_ref[...], a1_ref[...]])
        out = jnp.dot(a, b_ref[...].reshape(depth, cols), preferred_element_type=F32).astype(BF)
        o0[...] = out[:tok]
        o1[...] = out[tok:]

    return pl.pallas_call(
        kernel,
        out_shape=[jax.ShapeDtypeStruct((tok, cols), BF)] * 2,
        in_specs=[VMEM] * 3,
        out_specs=[VMEM] * 2,
        compiler_params=pltpu.CompilerParams(vmem_limit_bytes=8 * 2**20),
        cost_estimate=pl.CostEstimate(
            flops=4 * tok * depth * cols, bytes_accessed=4 * tok * depth + 2 * depth * cols, transcendentals=0
        ),
    )(a0, a1, whole)


def partials(g0, g1, p0, p1, pos):
    tok, ffw = g0.shape
    cols = p0.shape[1]
    nb = ffw // 16
    rows = nb // 4

    def kernel(pos_ref, g0_ref, g1_ref, p0_ref, p1_ref, *refs):
        outs, scratch = refs[:6], refs[6]
        dims = (((0,), (0,)), ((), ()))
        for i, run in enumerate(chips()):
            y, x = (absolute(*run[0], a, pos_ref, pos_ref[3]) for a in "yx")
            at = pl.ds(pl.multiple_of((y * 4 + x) * nb, nb), nb)
            scratch[i % 2] = (
                (
                    lax.dot_general(g0_ref[:, at], p0_ref[...], dims, preferred_element_type=F32)
                    + lax.dot_general(g1_ref[:, at], p1_ref[...], dims, preferred_element_type=F32)
                )
                .astype(BF)
                .reshape(4, rows, cols)
            )
            for u, v in run:
                part, w = part_of(v)
                first, second, third = (u[a] for a in ORDERS[part])
                outs[2 * part + first][second, third, w] = scratch[i % 2, absolute(u, v, "z", pos_ref, pos_ref[3])]

    shapes = [(2, 2, end - begin, rows, cols) for begin, end in PARTS for _ in range(2)]
    return pl.pallas_call(
        kernel,
        out_shape=[jax.ShapeDtypeStruct(s, BF) for s in shapes],
        in_specs=[SMEM] + [VMEM] * 4,
        out_specs=[VMEM] * 6,
        scratch_shapes=[pltpu.VMEM((2, 4, rows, cols), BF)],
        compiler_params=pltpu.CompilerParams(vmem_limit_bytes=24 * 2**20),
        cost_estimate=pl.CostEstimate(
            flops=4 * tok * ffw * cols, bytes_accessed=4 * tok * ffw + 2 * ffw * cols, transcendentals=0
        ),
    )(pos, g0, g1, p0, p1)


def updates(basis, own, other, core):
    rows, rank = basis.shape
    shard, half = own.shape[1:]
    nb = 4 * shard
    ffw = 16 * nb

    def kernel(core_ref, own_ref, other_ref, b_ref, out, stage, sem):
        dims = (((1,), (1,)), ((), ()))
        core = core_ref[0]
        copies = []
        for i in range(16):
            at = pl.ds(i * nb, nb)
            total = lax.dot_general(
                b_ref[core], own_ref[4 * i : 4 * i + 4].reshape(nb, half), dims, preferred_element_type=F32
            ) + lax.dot_general(
                b_ref[1 - core], other_ref[4 * i : 4 * i + 4].reshape(nb, half), dims, preferred_element_type=F32
            )
            stage[:, at] = (-galore_scale * total).astype(BF)
            copies.append(pltpu.make_async_copy(stage.at[:, at], out.at[:, at], sem.at[i]))
            copies[-1].start()
        for copy in copies:
            copy.wait()

    halves = jnp.stack([basis[:, :half], basis[:, half:]])
    return pl.pallas_call(
        kernel,
        out_shape=jax.ShapeDtypeStruct((rows, ffw), BF),
        in_specs=[SMEM] + [VMEM] * 3,
        out_specs=pl.BlockSpec(memory_space=pl.ANY),
        scratch_shapes=[pltpu.VMEM((rows, ffw), BF), pltpu.SemaphoreType.DMA((16,))],
        compiler_params=pltpu.CompilerParams(vmem_limit_bytes=12 * 2**20),
        cost_estimate=pl.CostEstimate(
            flops=2 * rows * ffw * rank, bytes_accessed=2 * (ffw * rank + rows * ffw), transcendentals=0
        ),
    )(core, own, other, halves)


def add(a, b):
    return (a.astype(F32) + b.astype(F32)).astype(BF)


def local(activations, out_grads, basis, first_moment, second_moment):
    core, zl = lax.axis_index("c"), lax.axis_index("zl")
    places = [lax.axis_index(a + "1") * 2 + lax.axis_index(a + "0") for a in "yx"] + [lax.axis_index("zh") * 2 + zl]
    pos = jnp.stack(places + [core]).astype(jnp.int32)
    rank = basis.shape[1]
    half = rank // 2
    shard = out_grads.shape[1] // 64
    brows = basis.shape[0] // 2

    act_other = swap_core(activations)
    g_other = swap_core(out_grads)

    at = (zl * shard, core * half)
    moments = jnp.stack([lax.dynamic_slice(m, at, (shard, half)) for m in (first_moment, second_moment)])

    mine, theirs = pos[3:], 1 - pos[3:]
    swapped = [lambda: ()] * 2 + [lambda: (act_other, g_other, moments)]
    near, far, (act_other, g_other, moments) = gather(
        lax.dynamic_slice(basis, (zl * brows, core * half), (brows, half)), swapped
    )
    whole = place(place(None, near, 0, pos, mine), far, 1, pos, mine)
    near_acts = load(activations, act_other)
    projected = project(*near_acts, whole)
    sums = partials(out_grads, g_other, *projected, pos)
    keeps, sends = sums[0::2], sums[1::2]

    moments = lax.optimization_barrier((moments, projected[0]))[0]

    for stage in range(3):
        gots = [swap(send, order[stage]) for order, send in zip(ORDERS, sends)]
        if stage == 1:
            *gots, theirs_moments = lax.optimization_barrier((*gots, swap(moments, "z", late=1)))
        if stage < 2:
            sends = [add(keep[1], got[1]) for keep, got in zip(keeps, gots)]
            keeps = [add(keep[0], got[0]) for keep, got in zip(keeps, gots)]
        else:
            keeps = [add(keep, got) for keep, got in zip(keeps, gots)]
    keep = jnp.concatenate(keeps).reshape(2, 2, 2, shard, half)
    gots = [swap(keep[vy, vx], axes, late=1) for vy, vx, axes in ((0, 1, "x"), (1, 0, "y"), (1, 1, "xy"))]
    keep = sum(term.astype(F32) for term in (keep[0, 0], *gots)).astype(BF)
    blocks = add(keep, swap(keep, "z", late=1)[::-1])
    reduced = blocks[0]

    def adam(first, second, red):
        new_first = beta_one * first + (1.0 - beta_one) * red
        new_second = beta_two * second + (1.0 - beta_two) * red * red
        return new_first, new_second

    new_first, new_second = adam(*jnp.stack([moments, theirs_moments], axis=1), blocks.astype(F32))
    corrected = new_first / (1.0 - beta_one**STEP)
    normalized = (corrected / (jnp.sqrt(new_second / (1.0 - beta_two**STEP)) + eps)).astype(BF)

    def columns():
        other = swap_core(reduced)
        both = jnp.concatenate([reduced, other], 1), jnp.concatenate([other, reduced], 1)
        return (jnp.where(core == 0, *both),)

    def rows(own):
        other = swap_low(own)
        return (jnp.where(zl == 0, jnp.concatenate([own, other]), jnp.concatenate([other, own])),)

    near, far, (rows,) = gather(normalized, [columns, rows])
    own = place(None, near, 0, pos, mine)
    near = lax.optimization_barrier((*near, own))[:3]
    other = place(None, [swap_core(a) for a in near], 0, pos, theirs)
    update = updates(
        basis, place(own, far, 1, pos, mine), place(other, [swap_core(a) for a in far], 1, pos, theirs), mine
    )
    out_first, out_second = adam(first_moment, second_moment, rows.astype(F32))
    return (update, out_first, out_second)


def solution(mesh):
    chips = Mesh(mesh.devices.reshape(2, 2, 2, 2, 2, 2, 2), AXES)
    in_specs = (P(AXES, None), P(AXES, None), P(FSDP, None), P(FSDP, None), P(FSDP, None))
    out_specs = (P(FSDP, None), P(FSDP, None), P(FSDP, None))
    return jax.shard_map(local, mesh=chips, in_specs=in_specs, out_specs=out_specs, check_vma=False)
```

```python
import itertools

import jax
import jax.numpy as jnp
from jax import lax
from jax.experimental import pallas as pl
from jax.experimental.pallas import tpu as pltpu
from jax.sharding import Mesh
from jax.sharding import PartitionSpec as P

STEP = 10


beta_one = 0.9
beta_two = 0.99
eps = 1e-08
galore_scale = 4.0

BF = jnp.bfloat16
F32 = jnp.float32
AXES = ("zl", "c", "y1", "y0", "x1", "x0", "zh")
FSDP = ("y1", "y0", "x1", "x0", "zh")
ORDERS = ("xyz", "yzx", "zxy")


def flat(co):
    return ((co["z"] % 2) * 2 + co["c"]) * 32 + (co["y"] * 4 + co["x"]) * 2 + co["z"] // 2


def permute(arr, move):
    pairs = []
    for c in range(2):
        for y in range(4):
            for x in range(4):
                for z in range(4):
                    co = {"c": c, "y": y, "x": x, "z": z}
                    pairs.append((flat(co), flat(move(dict(co)))))
    return lax.ppermute(arr, AXES, pairs)


def swap(arr, axes, late=0):
    def move(co):
        for axis in axes:
            co[axis] ^= 3 if co["c"] != late else 1
        return co

    return permute(arr, move)


def swap_core(arr):
    def move(co):
        co["c"] ^= 1
        return co

    return permute(arr, move)


def swap_low(arr):
    def move(co):
        co["z"] ^= 1
        return co

    return permute(arr, move)


PARTS = ((0, 3), (3, 6), (6, 8))


def join(arrays, gots, *extra):
    n = len(arrays)
    both = lax.optimization_barrier((*arrays, *gots, *extra))
    return [jnp.stack(pair) for pair in zip(both[:n], both[n : 2 * n])], *both[2 * n :]


def gather(piece, beside):
    tied = ()
    if piece.ndim == 2:
        ((piece,),) = join([piece], [swap(piece, "z", late=1)])
    gots = [swap(piece, axes, late=1) for axes in ("x", "y", "xy")]
    if beside:
        tied = beside[0](*tied)
    blocks = lax.optimization_barrier((piece, *gots, *tied))
    tied, beside = blocks[4:], beside[1:]
    piece = jnp.concatenate(blocks[:4])
    parts = [piece[begin:end] for begin, end in PARTS]
    for stage in (2, 1):
        gots = [swap(part, order[stage]) for order, part in zip(ORDERS, parts)]
        if beside:
            tied = beside[0](*tied)
        parts, *tied = join(parts, gots, *tied)
        beside = beside[1:]
    return parts, [swap(part, order[0]) for order, part in zip(ORDERS, parts)], tied


def bits(place, core):
    high = place // 2
    low = lax.bitwise_xor(place % 2, high)
    return low + core * (high - low), high + core * (low - high)


def place_of(u, v, core):
    high, low = v + core * (u - v), u + core * (v - u)
    return high * 2 + lax.bitwise_xor(high, low)


def chips():
    for uy, ux, vy, vx in itertools.product(range(2), repeat=4):
        yield [({"y": uy, "x": ux, "z": uz}, vy * 4 + vx * 2 + vz) for uz in range(2) for vz in range(2)]


def absolute(u, v, axis, pos_ref, core):
    j = "yxz".index(axis)
    return lax.bitwise_xor(pos_ref[j], place_of(u[axis], v // (4, 2, 1)[j] % 2, core))


def part_of(v):
    return next((i, v - begin) for i, (begin, end) in enumerate(PARTS) if v < end)


SMEM = pl.BlockSpec(memory_space=pltpu.SMEM)
VMEM = pl.BlockSpec(memory_space=pltpu.VMEM)
HBM = pl.BlockSpec(memory_space=pltpu.HBM)


def place(whole, arrays, which, pos, core):
    rows, cols = arrays[0].shape[-2:]
    size = 64 * rows * cols

    def kernel(pos_ref, core_ref, *refs):
        out = refs[-1]
        for run in chips():
            for u, v in run:
                part, w = part_of(v)
                first, second, third = (u[a] for a in ORDERS[part])
                if first == which:
                    y, x, z = (absolute(u, v, a, pos_ref, core_ref[0]) for a in "yxz")
                    out[(y * 4 + x) * 4 + z] = refs[part][second, third, w]

    return pl.pallas_call(
        kernel,
        out_shape=jax.ShapeDtypeStruct((64, rows, cols), BF),
        in_specs=[SMEM] * 2 + [VMEM] * (3 if whole is None else 4),
        out_specs=VMEM,
        input_output_aliases={} if whole is None else {5: 0},
        compiler_params=pltpu.CompilerParams(vmem_limit_bytes=8 * 2**20),
        cost_estimate=pl.CostEstimate(flops=0, bytes_accessed=2 * size, transcendentals=0),
    )(pos, core, *arrays, *(() if whole is None else (whole,)))


def load(*arrays):
    n, cuts = len(arrays), 4

    def kernel(*refs):
        sem = refs[-1]
        copies = []
        for src, dst in zip(refs[:n], refs[n:]):
            rows = src.shape[0] // cuts
            for i in range(cuts):
                at = pl.ds(i * rows, rows)
                copies.append(pltpu.make_async_copy(src.at[at], dst.at[at], sem.at[len(copies)]))
        for copy in copies:
            copy.start()
        for copy in copies:
            copy.wait()

    return pl.pallas_call(
        kernel,
        out_shape=[jax.ShapeDtypeStruct(a.shape, a.dtype) for a in arrays],
        in_specs=[HBM] * n,
        out_specs=[VMEM] * n,
        scratch_shapes=[pltpu.SemaphoreType.DMA((n * cuts,))],
        compiler_params=pltpu.CompilerParams(vmem_limit_bytes=8 * 2**20),
        cost_estimate=pl.CostEstimate(flops=0, bytes_accessed=sum(2 * a.size for a in arrays), transcendentals=0),
    )(*arrays)


def project(a0, a1, whole):
    tok, depth = a0.shape
    cols = whole.shape[2]

    def kernel(a0_ref, a1_ref, b_ref, o0, o1):
        a = jnp.concatenate([a0_ref[...], a1_ref[...]])
        out = jnp.dot(a, b_ref[...].reshape(depth, cols), preferred_element_type=F32).astype(BF)
        o0[...] = out[:tok]
        o1[...] = out[tok:]

    return pl.pallas_call(
        kernel,
        out_shape=[jax.ShapeDtypeStruct((tok, cols), BF)] * 2,
        in_specs=[VMEM] * 3,
        out_specs=[VMEM] * 2,
        compiler_params=pltpu.CompilerParams(vmem_limit_bytes=8 * 2**20),
        cost_estimate=pl.CostEstimate(
            flops=4 * tok * depth * cols, bytes_accessed=4 * tok * depth + 2 * depth * cols, transcendentals=0
        ),
    )(a0, a1, whole)


def partials(g0, g1, p0, p1, pos):
    tok, ffw = g0.shape
    cols = p0.shape[1]
    nb = ffw // 16
    rows = nb // 4

    def kernel(pos_ref, g0_ref, g1_ref, p0_ref, p1_ref, *refs):
        outs, scratch = refs[:6], refs[6]
        dims = (((0,), (0,)), ((), ()))
        for i, run in enumerate(chips()):
            y, x = (absolute(*run[0], a, pos_ref, pos_ref[3]) for a in "yx")
            at = pl.ds(pl.multiple_of((y * 4 + x) * nb, nb), nb)
            scratch[i % 2] = (
                (
                    lax.dot_general(g0_ref[:, at], p0_ref[...], dims, preferred_element_type=F32)
                    + lax.dot_general(g1_ref[:, at], p1_ref[...], dims, preferred_element_type=F32)
                )
                .astype(BF)
                .reshape(4, rows, cols)
            )
            for u, v in run:
                part, w = part_of(v)
                first, second, third = (u[a] for a in ORDERS[part])
                outs[2 * part + first][second, third, w] = scratch[i % 2, absolute(u, v, "z", pos_ref, pos_ref[3])]

    shapes = [(2, 2, end - begin, rows, cols) for begin, end in PARTS for _ in range(2)]
    return pl.pallas_call(
        kernel,
        out_shape=[jax.ShapeDtypeStruct(s, BF) for s in shapes],
        in_specs=[SMEM] + [VMEM] * 4,
        out_specs=[VMEM] * 6,
        scratch_shapes=[pltpu.VMEM((2, 4, rows, cols), BF)],
        compiler_params=pltpu.CompilerParams(vmem_limit_bytes=24 * 2**20),
        cost_estimate=pl.CostEstimate(
            flops=4 * tok * ffw * cols, bytes_accessed=4 * tok * ffw + 2 * ffw * cols, transcendentals=0
        ),
    )(pos, g0, g1, p0, p1)


def updates(basis, own, other, core):
    rows, rank = basis.shape
    shard, half = own.shape[1:]
    nb = 4 * shard
    ffw = 16 * nb

    def kernel(core_ref, own_ref, other_ref, b_ref, out, stage, sem):
        dims = (((1,), (1,)), ((), ()))
        core = core_ref[0]
        copies = []
        for i in range(16):
            at = pl.ds(i * nb, nb)
            total = lax.dot_general(
                b_ref[core], own_ref[4 * i : 4 * i + 4].reshape(nb, half), dims, preferred_element_type=F32
            ) + lax.dot_general(
                b_ref[1 - core], other_ref[4 * i : 4 * i + 4].reshape(nb, half), dims, preferred_element_type=F32
            )
            stage[:, at] = (-galore_scale * total).astype(BF)
            copies.append(pltpu.make_async_copy(stage.at[:, at], out.at[:, at], sem.at[i]))
            copies[-1].start()
        for copy in copies:
            copy.wait()

    halves = jnp.stack([basis[:, :half], basis[:, half:]])
    return pl.pallas_call(
        kernel,
        out_shape=jax.ShapeDtypeStruct((rows, ffw), BF),
        in_specs=[SMEM] + [VMEM] * 3,
        out_specs=pl.BlockSpec(memory_space=pl.ANY),
        scratch_shapes=[pltpu.VMEM((rows, ffw), BF), pltpu.SemaphoreType.DMA((16,))],
        compiler_params=pltpu.CompilerParams(vmem_limit_bytes=12 * 2**20),
        cost_estimate=pl.CostEstimate(
            flops=2 * rows * ffw * rank, bytes_accessed=2 * (ffw * rank + rows * ffw), transcendentals=0
        ),
    )(core, own, other, halves)


def add(a, b):
    return (a.astype(F32) + b.astype(F32)).astype(BF)


def local(activations, out_grads, basis, first_moment, second_moment):
    core, zl = lax.axis_index("c"), lax.axis_index("zl")
    places = [lax.axis_index(a + "1") * 2 + lax.axis_index(a + "0") for a in "yx"] + [lax.axis_index("zh") * 2 + zl]
    pos = jnp.stack(places + [core]).astype(jnp.int32)
    rank = basis.shape[1]
    half = rank // 2
    shard = out_grads.shape[1] // 64
    brows = basis.shape[0] // 2

    act_other = swap_core(activations)
    g_other = swap_core(out_grads)

    at = (zl * shard, core * half)
    moments = jnp.stack([lax.dynamic_slice(m, at, (shard, half)) for m in (first_moment, second_moment)])

    mine, theirs = pos[3:], 1 - pos[3:]
    swapped = [lambda: ()] * 2 + [lambda: (act_other, g_other, moments)]
    near, far, (act_other, g_other, moments) = gather(
        lax.dynamic_slice(basis, (zl * brows, core * half), (brows, half)), swapped
    )
    whole = place(place(None, near, 0, pos, mine), far, 1, pos, mine)
    act_other, g_other = load(act_other, g_other)
    projected = project(activations, act_other, whole)
    sums = partials(out_grads, g_other, *projected, pos)
    keeps, sends = sums[0::2], sums[1::2]

    moments = lax.optimization_barrier((moments, projected[0]))[0]

    for stage in range(3):
        gots = [swap(send, order[stage]) for order, send in zip(ORDERS, sends)]
        if stage == 1:
            gots[2], theirs_moments = lax.optimization_barrier((gots[2], swap(moments, "z", late=1)))
        if stage < 2:
            sends = [add(keep[1], got[1]) for keep, got in zip(keeps, gots)]
            keeps = [add(keep[0], got[0]) for keep, got in zip(keeps, gots)]
        else:
            keeps = [add(keep, got) for keep, got in zip(keeps, gots)]
    keep = jnp.concatenate(keeps).reshape(2, 2, 2, shard, half)
    gots = [swap(keep[vy, vx], axes, late=1) for vy, vx, axes in ((0, 1, "x"), (1, 0, "y"), (1, 1, "xy"))]
    keep = sum(term.astype(F32) for term in (keep[0, 0], *gots)).astype(BF)
    blocks = add(keep, swap(keep, "z", late=1)[::-1])
    reduced = blocks[0]

    def adam(first, second, red):
        new_first = beta_one * first + (1.0 - beta_one) * red
        new_second = beta_two * second + (1.0 - beta_two) * red * red
        return new_first, new_second

    new_first, new_second = adam(*jnp.stack([moments, theirs_moments], axis=1), blocks.astype(F32))
    corrected = new_first / (1.0 - beta_one**STEP)
    normalized = (corrected / (jnp.sqrt(new_second / (1.0 - beta_two**STEP)) + eps)).astype(BF)

    def columns():
        other = swap_core(reduced)
        both = jnp.concatenate([reduced, other], 1), jnp.concatenate([other, reduced], 1)
        return (jnp.where(core == 0, *both),)

    def rows(own):
        other = swap_low(own)
        return (jnp.where(zl == 0, jnp.concatenate([own, other]), jnp.concatenate([other, own])),)

    near, far, (rows,) = gather(normalized, [columns, rows])
    own = place(None, near, 0, pos, mine)
    near = lax.optimization_barrier((*near, own))[:3]
    other = place(None, [swap_core(a) for a in near], 0, pos, theirs)
    update = updates(
        basis, place(own, far, 1, pos, mine), place(other, [swap_core(a) for a in far], 1, pos, theirs), mine
    )
    out_first, out_second = adam(first_moment, second_moment, rows.astype(F32))
    return (update, out_first, out_second)


def solution(mesh):
    chips = Mesh(mesh.devices.reshape(2, 2, 2, 2, 2, 2, 2), AXES)
    in_specs = (P(AXES, None), P(AXES, None), P(FSDP, None), P(FSDP, None), P(FSDP, None))
    out_specs = (P(FSDP, None), P(FSDP, None), P(FSDP, None))
    return jax.shard_map(local, mesh=chips, in_specs=in_specs, out_specs=out_specs, check_vma=False)
```

```python
import itertools

import jax
import jax.numpy as jnp
from jax import lax
from jax.experimental import pallas as pl
from jax.experimental.pallas import tpu as pltpu
from jax.sharding import Mesh
from jax.sharding import PartitionSpec as P

STEP = 10


beta_one = 0.9
beta_two = 0.99
eps = 1e-08
galore_scale = 4.0

BF = jnp.bfloat16
F32 = jnp.float32
AXES = ("zl", "c", "y1", "y0", "x1", "x0", "zh")
FSDP = ("y1", "y0", "x1", "x0", "zh")
ORDERS = ("xyz", "yzx", "zxy")


def flat(co):
    return ((co["z"] % 2) * 2 + co["c"]) * 32 + (co["y"] * 4 + co["x"]) * 2 + co["z"] // 2


def permute(arr, move):
    pairs = []
    for c in range(2):
        for y in range(4):
            for x in range(4):
                for z in range(4):
                    co = {"c": c, "y": y, "x": x, "z": z}
                    pairs.append((flat(co), flat(move(dict(co)))))
    return lax.ppermute(arr, AXES, pairs)


def swap(arr, axes, late=0):
    def move(co):
        for axis in axes:
            co[axis] ^= 3 if co["c"] != late else 1
        return co

    return permute(arr, move)


def swap_core(arr):
    def move(co):
        co["c"] ^= 1
        return co

    return permute(arr, move)


def swap_low(arr):
    def move(co):
        co["z"] ^= 1
        return co

    return permute(arr, move)


PARTS = ((0, 3), (3, 6), (6, 8))


def join(arrays, gots, *extra):
    n = len(arrays)
    both = lax.optimization_barrier((*arrays, *gots, *extra))
    return [jnp.stack(pair) for pair in zip(both[:n], both[n : 2 * n])], *both[2 * n :]


def gather(piece, beside):
    tied = ()
    if piece.ndim == 2:
        ((piece,),) = join([piece], [swap(piece, "z", late=1)])
    gots = [swap(piece, axes, late=1) for axes in ("xy", "x", "y")]
    if beside:
        tied = beside[0](*tied)
    blocks = lax.optimization_barrier((piece, *gots, *tied))
    tied, beside = blocks[4:], beside[1:]
    piece = jnp.concatenate([blocks[0], blocks[2], blocks[3], blocks[1]])
    parts = [piece[begin:end] for begin, end in PARTS]
    for stage in (2, 1):
        gots = [swap(part, order[stage]) for order, part in zip(ORDERS, parts)]
        if beside:
            tied = beside[0](*tied)
        parts, *tied = join(parts, gots, *tied)
        beside = beside[1:]
    return parts, [swap(part, order[0]) for order, part in zip(ORDERS, parts)], tied


def bits(place, core):
    high = place // 2
    low = lax.bitwise_xor(place % 2, high)
    return low + core * (high - low), high + core * (low - high)


def place_of(u, v, core):
    high, low = v + core * (u - v), u + core * (v - u)
    return high * 2 + lax.bitwise_xor(high, low)


def chips():
    for uy, ux, vy, vx in itertools.product(range(2), repeat=4):
        yield [({"y": uy, "x": ux, "z": uz}, vy * 4 + vx * 2 + vz) for uz in range(2) for vz in range(2)]


def absolute(u, v, axis, pos_ref, core):
    j = "yxz".index(axis)
    return lax.bitwise_xor(pos_ref[j], place_of(u[axis], v // (4, 2, 1)[j] % 2, core))


def part_of(v):
    return next((i, v - begin) for i, (begin, end) in enumerate(PARTS) if v < end)


SMEM = pl.BlockSpec(memory_space=pltpu.SMEM)
VMEM = pl.BlockSpec(memory_space=pltpu.VMEM)
HBM = pl.BlockSpec(memory_space=pltpu.HBM)


def place(whole, arrays, which, pos, core):
    rows, cols = arrays[0].shape[-2:]
    size = 64 * rows * cols

    def kernel(pos_ref, core_ref, *refs):
        out = refs[-1]
        for run in chips():
            for u, v in run:
                part, w = part_of(v)
                first, second, third = (u[a] for a in ORDERS[part])
                if first == which:
                    y, x, z = (absolute(u, v, a, pos_ref, core_ref[0]) for a in "yxz")
                    out[(y * 4 + x) * 4 + z] = refs[part][second, third, w]

    return pl.pallas_call(
        kernel,
        out_shape=jax.ShapeDtypeStruct((64, rows, cols), BF),
        in_specs=[SMEM] * 2 + [VMEM] * (3 if whole is None else 4),
        out_specs=VMEM,
        input_output_aliases={} if whole is None else {5: 0},
        compiler_params=pltpu.CompilerParams(vmem_limit_bytes=8 * 2**20),
        cost_estimate=pl.CostEstimate(flops=0, bytes_accessed=2 * size, transcendentals=0),
    )(pos, core, *arrays, *(() if whole is None else (whole,)))


def load(*arrays):
    n, cuts = len(arrays), 4

    def kernel(*refs):
        sem = refs[-1]
        copies = []
        for src, dst in zip(refs[:n], refs[n:]):
            rows = src.shape[0] // cuts
            for i in range(cuts):
                at = pl.ds(i * rows, rows)
                copies.append(pltpu.make_async_copy(src.at[at], dst.at[at], sem.at[len(copies)]))
        for copy in copies:
            copy.start()
        for copy in copies:
            copy.wait()

    return pl.pallas_call(
        kernel,
        out_shape=[jax.ShapeDtypeStruct(a.shape, a.dtype) for a in arrays],
        in_specs=[HBM] * n,
        out_specs=[VMEM] * n,
        scratch_shapes=[pltpu.SemaphoreType.DMA((n * cuts,))],
        compiler_params=pltpu.CompilerParams(vmem_limit_bytes=8 * 2**20),
        cost_estimate=pl.CostEstimate(flops=0, bytes_accessed=sum(2 * a.size for a in arrays), transcendentals=0),
    )(*arrays)


def project(a0, a1, whole):
    tok, depth = a0.shape
    cols = whole.shape[2]

    def kernel(a0_ref, a1_ref, b_ref, o0, o1):
        a = jnp.concatenate([a0_ref[...], a1_ref[...]])
        out = jnp.dot(a, b_ref[...].reshape(depth, cols), preferred_element_type=F32).astype(BF)
        o0[...] = out[:tok]
        o1[...] = out[tok:]

    return pl.pallas_call(
        kernel,
        out_shape=[jax.ShapeDtypeStruct((tok, cols), BF)] * 2,
        in_specs=[VMEM] * 3,
        out_specs=[VMEM] * 2,
        compiler_params=pltpu.CompilerParams(vmem_limit_bytes=8 * 2**20),
        cost_estimate=pl.CostEstimate(
            flops=4 * tok * depth * cols, bytes_accessed=4 * tok * depth + 2 * depth * cols, transcendentals=0
        ),
    )(a0, a1, whole)


def partials(g0, g1, p0, p1, pos):
    tok, ffw = g0.shape
    cols = p0.shape[1]
    nb = ffw // 16
    rows = nb // 4

    def kernel(pos_ref, g0_ref, g1_ref, p0_ref, p1_ref, *refs):
        outs, scratch = refs[:6], refs[6]
        dims = (((0,), (0,)), ((), ()))
        for i, run in enumerate(chips()):
            y, x = (absolute(*run[0], a, pos_ref, pos_ref[3]) for a in "yx")
            at = pl.ds(pl.multiple_of((y * 4 + x) * nb, nb), nb)
            scratch[i % 2] = (
                (
                    lax.dot_general(g0_ref[:, at], p0_ref[...], dims, preferred_element_type=F32)
                    + lax.dot_general(g1_ref[:, at], p1_ref[...], dims, preferred_element_type=F32)
                )
                .astype(BF)
                .reshape(4, rows, cols)
            )
            for u, v in run:
                part, w = part_of(v)
                first, second, third = (u[a] for a in ORDERS[part])
                outs[2 * part + first][second, third, w] = scratch[i % 2, absolute(u, v, "z", pos_ref, pos_ref[3])]

    shapes = [(2, 2, end - begin, rows, cols) for begin, end in PARTS for _ in range(2)]
    return pl.pallas_call(
        kernel,
        out_shape=[jax.ShapeDtypeStruct(s, BF) for s in shapes],
        in_specs=[SMEM] + [VMEM] * 4,
        out_specs=[VMEM] * 6,
        scratch_shapes=[pltpu.VMEM((2, 4, rows, cols), BF)],
        compiler_params=pltpu.CompilerParams(vmem_limit_bytes=24 * 2**20),
        cost_estimate=pl.CostEstimate(
            flops=4 * tok * ffw * cols, bytes_accessed=4 * tok * ffw + 2 * ffw * cols, transcendentals=0
        ),
    )(pos, g0, g1, p0, p1)


def updates(basis, own, other, core):
    rows, rank = basis.shape
    shard, half = own.shape[1:]
    nb = 4 * shard
    ffw = 16 * nb

    def kernel(core_ref, own_ref, other_ref, b_ref, out, stage, sem):
        dims = (((1,), (1,)), ((), ()))
        core = core_ref[0]
        copies = []
        for i in range(16):
            at = pl.ds(i * nb, nb)
            total = lax.dot_general(
                b_ref[core], own_ref[4 * i : 4 * i + 4].reshape(nb, half), dims, preferred_element_type=F32
            ) + lax.dot_general(
                b_ref[1 - core], other_ref[4 * i : 4 * i + 4].reshape(nb, half), dims, preferred_element_type=F32
            )
            stage[:, at] = (-galore_scale * total).astype(BF)
            copies.append(pltpu.make_async_copy(stage.at[:, at], out.at[:, at], sem.at[i]))
            copies[-1].start()
        for copy in copies:
            copy.wait()

    halves = jnp.stack([basis[:, :half], basis[:, half:]])
    return pl.pallas_call(
        kernel,
        out_shape=jax.ShapeDtypeStruct((rows, ffw), BF),
        in_specs=[SMEM] + [VMEM] * 3,
        out_specs=pl.BlockSpec(memory_space=pl.ANY),
        scratch_shapes=[pltpu.VMEM((rows, ffw), BF), pltpu.SemaphoreType.DMA((16,))],
        compiler_params=pltpu.CompilerParams(vmem_limit_bytes=12 * 2**20),
        cost_estimate=pl.CostEstimate(
            flops=2 * rows * ffw * rank, bytes_accessed=2 * (ffw * rank + rows * ffw), transcendentals=0
        ),
    )(core, own, other, halves)


def add(a, b):
    return (a.astype(F32) + b.astype(F32)).astype(BF)


def local(activations, out_grads, basis, first_moment, second_moment):
    core, zl = lax.axis_index("c"), lax.axis_index("zl")
    places = [lax.axis_index(a + "1") * 2 + lax.axis_index(a + "0") for a in "yx"] + [lax.axis_index("zh") * 2 + zl]
    pos = jnp.stack(places + [core]).astype(jnp.int32)
    rank = basis.shape[1]
    half = rank // 2
    shard = out_grads.shape[1] // 64
    brows = basis.shape[0] // 2

    act_other = swap_core(activations)
    g_other = swap_core(out_grads)

    at = (zl * shard, core * half)
    moments = jnp.stack([lax.dynamic_slice(m, at, (shard, half)) for m in (first_moment, second_moment)])

    mine, theirs = pos[3:], 1 - pos[3:]
    swapped = [lambda: ()] * 2 + [lambda: (act_other, g_other, moments)]
    near, far, (act_other, g_other, moments) = gather(
        lax.dynamic_slice(basis, (zl * brows, core * half), (brows, half)), swapped
    )
    whole = place(place(None, near, 0, pos, mine), far, 1, pos, mine)
    act_other, g_other = load(act_other, g_other)
    projected = project(activations, act_other, whole)
    sums = partials(out_grads, g_other, *projected, pos)
    keeps, sends = sums[0::2], sums[1::2]

    moments = lax.optimization_barrier((moments, projected[0]))[0]

    for stage in range(3):
        gots = [swap(send, order[stage]) for order, send in zip(ORDERS, sends)]
        if stage == 1:
            gots[2], theirs_moments = lax.optimization_barrier((gots[2], swap(moments, "z", late=1)))
        if stage < 2:
            sends = [add(keep[1], got[1]) for keep, got in zip(keeps, gots)]
            keeps = [add(keep[0], got[0]) for keep, got in zip(keeps, gots)]
        else:
            keeps = [add(keep, got) for keep, got in zip(keeps, gots)]
    keep = jnp.concatenate(keeps).reshape(2, 2, 2, shard, half)
    gots = [swap(keep[vy, vx], axes, late=1) for vy, vx, axes in ((0, 1, "x"), (1, 0, "y"), (1, 1, "xy"))]
    keep = sum(term.astype(F32) for term in (keep[0, 0], *gots)).astype(BF)
    blocks = add(keep, swap(keep, "z", late=1)[::-1])
    reduced = blocks[0]

    def adam(first, second, red):
        new_first = beta_one * first + (1.0 - beta_one) * red
        new_second = beta_two * second + (1.0 - beta_two) * red * red
        return new_first, new_second

    new_first, new_second = adam(*jnp.stack([moments, theirs_moments], axis=1), blocks.astype(F32))
    corrected = new_first / (1.0 - beta_one**STEP)
    normalized = (corrected / (jnp.sqrt(new_second / (1.0 - beta_two**STEP)) + eps)).astype(BF)

    def columns():
        other = swap_core(reduced)
        both = jnp.concatenate([reduced, other], 1), jnp.concatenate([other, reduced], 1)
        return (jnp.where(core == 0, *both),)

    def rows(own):
        other = swap_low(own)
        return (jnp.where(zl == 0, jnp.concatenate([own, other]), jnp.concatenate([other, own])),)

    near, far, (rows,) = gather(normalized, [columns, rows])
    own = place(None, near, 0, pos, mine)
    near = lax.optimization_barrier((*near, own))[:3]
    other = place(None, [swap_core(a) for a in near], 0, pos, theirs)
    update = updates(
        basis, place(own, far, 1, pos, mine), place(other, [swap_core(a) for a in far], 1, pos, theirs), mine
    )
    out_first, out_second = adam(first_moment, second_moment, rows.astype(F32))
    return (update, out_first, out_second)


def solution(mesh):
    chips = Mesh(mesh.devices.reshape(2, 2, 2, 2, 2, 2, 2), AXES)
    in_specs = (P(AXES, None), P(AXES, None), P(FSDP, None), P(FSDP, None), P(FSDP, None))
    out_specs = (P(FSDP, None), P(FSDP, None), P(FSDP, None))
    return jax.shard_map(local, mesh=chips, in_specs=in_specs, out_specs=out_specs, check_vma=False)
```
